32 devices in a mesh: layers: 2 (over x), col: 16 (over z, y, core).
Axes of the slice: x: 2, y: 2, z: 4, core: 2. Of those that a mesh axis runs over, the one named last changes fastest.
Arguments:
- dense_weight: float32 [64, 16384], P('layers', 'col'), parts along dimension 0, may hold values from -6 to 6
- start_weight: float32 [64, 16384], P('layers', 'col'), parts along dimension 0, may hold values from -6 to 6
- keep_mask: int32 [64, 16384], P('layers', 'col'), parts along dimension 0, may hold values 0 or 1
- tile_plan: int32 [1056, 2], P(('layers', 'col')), parts along dimension 0, may hold values from 0 to 31, as said below
- hess_tiles: float32 [1056, 512, 512], P(('layers', 'col')), parts along dimension 0, as said below
Outputs:
- weights_out: float32 [64, 16384], P('layers', 'col'), parts along dimension 0
- velocity_out: float32 [64, 16384], P('layers', 'col'), parts along dimension 0
The draws below stay inside these ranges and needn't reach their ends.
There are 2 independent parts, one for each index of `layers`. The reference program is written for one: setup_inputs(seed, part) draws one part's arguments, and reference() takes and returns one part's arrays. A program takes and returns all parts, laid end to end along the dimension named above; each array names one. Nothing has to cross between parts.
Inputs may be any that keep to these rules, and one draw needn't show every extreme that they name: `tile_plan`: each live slot names a tile (a, b) with a >= b, and each of the 32 (33) / 2 lower-triangle tiles is named by exactly one slot; the other slots name (0, 0). `hess_tiles`: the tiles of a symmetric positive definite matrix at the places that tile_plan names; slots that name no tile hold zeros.
All inputs are finite; a program needn't handle non-finite values. No bound on the sum of `keep_mask` on one device may be relied on, other than what follows from the above.
Results may differ from the reference program's by a relative error of at most 0.0001.
Values sent between devices are 32-bit elements; how exact they have to be, the bound alone decides.
No kernel may reach another device: no remote copies, remote signals or barrier semaphores. Data moves between devices by JAX's collectives and lax.ppermute only.
A program may use at most 64 MiB of HBM per device.

```python
import math
import jax
import jax.numpy as jnp
from jax import lax

K = 16384
TB = 512
R = 32
ITERS = 2
NB = 32
PLAN_ROWS = 528


def plan_parts(key):
    order = jax.random.permutation(jax.random.fold_in(key, 11), PLAN_ROWS).astype(jnp.int32)
    count = NB * (NB + 1) // 2
    live = order < count
    index = jnp.where(live, order, 0)
    blocks = jnp.arange(NB, dtype=jnp.int32)
    starts = blocks * (blocks + 1) // 2
    row_of = jnp.sum((starts[None, :] <= index[:, None]).astype(jnp.int32), axis=1) - 1
    col_of = index - row_of * (row_of + 1) // 2
    return (row_of.astype(jnp.int32), col_of.astype(jnp.int32), live)


def draw_tile_plan(key, part):
    row_of, col_of, live = plan_parts(key)
    return jnp.stack([row_of, col_of], axis=1).astype(jnp.int32)


def draw_hess_tiles(key, part):
    row_of, col_of, live = plan_parts(key)
    noise_key = jax.random.fold_in(key, 23)
    diag_key = jax.random.fold_in(key, 29)
    raw = jax.random.normal(noise_key, (PLAN_ROWS, TB, TB), jnp.float32)
    raw = raw / math.sqrt(K)
    sym = (raw + jnp.swapaxes(raw, 1, 2)) / math.sqrt(2.0)
    diag_vals = jnp.exp(jax.random.uniform(diag_key, (PLAN_ROWS, TB), jnp.float32, math.log(2.0), math.log(4.0)))
    eye = jnp.eye(TB, dtype=jnp.float32)
    diag_tile = sym + eye[None, :, :] * diag_vals[:, :, None]
    same = (row_of == col_of)[:, None, None]
    tile = jnp.where(same, diag_tile, raw)
    return tile * live[:, None, None].astype(jnp.float32)


def plant(entries, key, least, largest):
    longest = entries.shape.index(max(entries.shape))
    spots = []
    for shift in (0, 1):
        where = [jax.random.randint(jax.random.fold_in(key, axis), (), 0, length) for axis, length in enumerate(entries.shape)]
        where[longest] = (where[longest] + shift) % entries.shape[longest]
        spots.append(tuple(where))
    return entries.at[spots[0]].set(least).at[spots[1]].set(largest)


def levels(rng, shape, cuts, smallest, largest):
    gain, own = 1.0, jax.random.fold_in(rng, 6)
    for dim, parts in cuts:
        steps = jnp.exp(jax.random.uniform(jax.random.fold_in(own, dim), (parts,), jnp.float32, smallest / len(cuts), largest / len(cuts)))
        gain = gain * jnp.repeat(steps, shape[dim] // parts).reshape([-1 if axis == dim else 1 for axis in range(len(shape))])
    return gain


def gaussian(rng, dims, width, most, pieces=(), kind=jnp.bfloat16):
    array = width * jax.random.normal(rng, dims, jnp.float32)
    if pieces:
        array = array * levels(rng, dims, pieces, -0.22, 0.18)
    return jnp.clip(array, -most, most).astype(kind)


def setup_inputs(seed: int = 0, part: int = 0) -> dict:
    key_list = jax.random.split(jax.random.key(seed), 6)
    part_splits = jax.random.split(jax.random.fold_in(key_list[5], part), 6)
    dense_weight = gaussian(part_splits[0], (R, K), 1.0, 6.0, ((1, 16),), jnp.float32)
    start_weight = gaussian(part_splits[1], (R, K), 1.0, 6.0, ((1, 16),), jnp.float32)
    keep_mask = plant((jax.random.randint(part_splits[2], (R, K), 0, 2) < 1).astype(jnp.int32), jax.random.fold_in(part_splits[2], 1), 0, 1)
    tile_plan = draw_tile_plan(jax.random.fold_in(jax.random.fold_in(key_list[5], part), 71), part)
    hess_tiles = draw_hess_tiles(jax.random.fold_in(jax.random.fold_in(key_list[5], part), 71), part)
    return dict(dense_weight=dense_weight, start_weight=start_weight, keep_mask=keep_mask, tile_plan=tile_plan, hess_tiles=hess_tiles)


step_size = 0.15
momentum = 0.6


def hessian_product(error, tile_plan, hess_tiles):
    order = hess_tiles.shape[1]
    gradient = jnp.zeros(error.shape, jnp.float32)

    def one_slot(slot, acc):
        row_block = tile_plan[slot, 0]
        col_block = tile_plan[slot, 1]
        tile = hess_tiles[slot]
        left = lax.dynamic_slice_in_dim(error, row_block * order, order, 1)
        right = lax.dynamic_slice_in_dim(error, col_block * order, order, 1)
        lower = jnp.dot(left, tile, precision=lax.Precision.HIGHEST, preferred_element_type=jnp.float32)
        upper = lax.dot_general(right, tile, (((1,), (1,)), ((), ())), precision=lax.Precision.HIGHEST, preferred_element_type=jnp.float32)
        factor = (row_block != col_block).astype(jnp.float32)
        current = lax.dynamic_slice_in_dim(acc, col_block * order, order, 1)
        acc = lax.dynamic_update_slice_in_dim(acc, current + lower, col_block * order, 1)
        current = lax.dynamic_slice_in_dim(acc, row_block * order, order, 1)
        acc = lax.dynamic_update_slice_in_dim(acc, current + factor * upper, row_block * order, 1)
        return acc

    return lax.fori_loop(0, tile_plan.shape[0], one_slot, gradient)


def reference(dense_weight, start_weight, keep_mask, tile_plan, hess_tiles):
    keep = keep_mask.astype(jnp.float32)
    weights = start_weight
    velocity = jnp.zeros(start_weight.shape, jnp.float32)
    for step in range(ITERS):
        error = weights - dense_weight
        gradient = hessian_product(error, tile_plan, hess_tiles)
        velocity = momentum * velocity + gradient
        weights = keep * (weights - step_size * velocity)
    return weights, velocity
```

```python
import functools

import jax
import jax.numpy as jnp
from jax import lax
from jax.experimental import pallas as pl
from jax.experimental.pallas import tpu as pltpu
from jax.sharding import PartitionSpec as P

ITERS = 2
MIB = 2**20

step_size = 0.15
momentum = 0.6

IN_VMEM = pl.BlockSpec(memory_space=pltpu.VMEM)


def stages_of(count):
    bits = [1 << i for i in range(count.bit_length() - 1)]
    near, far = bits[:2], bits[2:]
    groups = [far[i : i + 2] for i in range(0, len(far), 2)]
    return groups[::-1] + [[b] for b in near[::-1]]


def masks_of(group):
    masks = [0]
    for bit in group:
        masks += [m | bit for m in masks]
    return masks[1:]


def swap(x, mask):
    count = lax.axis_size("col")
    return lax.ppermute(x, "col", [(i, i ^ mask) for i in range(count)])


def gather(own):
    pieces = {0: own}
    for group in stages_of(lax.axis_size("col")):
        held = list(pieces)
        for mask in reversed(masks_of(group)):
            for p in held:
                pieces[p | mask] = swap(pieces[p], mask)
    return [pieces[p] for p in range(len(pieces))]


def scatter_sum(parts):
    held = dict(enumerate(parts))
    for group in reversed(stages_of(len(parts))):
        masks = masks_of(group)
        every = sum(group)
        kept = [p for p in held if not p & every]
        terms = {p: [held[p]] for p in kept}
        for p in reversed(kept):
            for mask in reversed(masks):
                terms[p].append(swap(held[p | mask], mask))
        if kept == [0]:
            return terms[0]
        held = {p: sum(terms[p][1:], terms[p][0]) for p in kept}


def split_kernel(tile_ref, split_ref):
    step = pl.program_id(0)
    for j in range(tile_ref.shape[0]):
        tile = tile_ref[j]
        high = tile.astype(jnp.bfloat16)
        slot = step * tile_ref.shape[0] + j
        split_ref[slot, 0] = high
        split_ref[slot, 1] = (tile - high.astype(jnp.float32)).astype(jnp.bfloat16)


def split_tiles(tiles):
    slots, order, _ = tiles.shape
    together = 3 if slots % 3 == 0 else 1
    return pl.pallas_call(
        split_kernel,
        grid=(slots // together,),
        in_specs=[pl.BlockSpec((together, order, order), lambda i: (i, 0, 0))],
        out_specs=IN_VMEM,
        out_shape=pltpu.VMEM((slots, 2, order, order), jnp.bfloat16),
        compiler_params=pltpu.CompilerParams(vmem_limit_bytes=16 * MIB),
        cost_estimate=pl.CostEstimate(flops=0, bytes_accessed=slots * order * order * 4, transcendentals=0),
        name="split_tiles",
    )(tiles)


def places(owner, order, width):
    if width >= order:
        each = width // order
        return [(slice(j * order, (j + 1) * order), owner * each + j, slice(None)) for j in range(each)]
    each = order // width
    start = pl.multiple_of(lax.rem(owner, each) * width, width)
    return [(slice(None), lax.div(owner, each), pl.ds(start, width))]


def product_kernel(count, plan, split, *refs):
    ins, outs, (err, acc) = refs[:count], refs[count : 2 * count], refs[2 * count :]
    blocks, rows, order = acc.shape
    width = ins[0].shape[1]
    me = lax.axis_index("col")
    for p in range(count):
        for part, block, columns in places(me ^ p, order, width):
            piece = ins[p][:, part]
            high = piece.astype(jnp.bfloat16)
            err[block, :rows, columns] = high
            err[block, rows:, columns] = (piece - high.astype(jnp.float32)).astype(jnp.bfloat16)
    acc[...] = jnp.zeros(acc.shape, jnp.float32)

    def one_slot(slot, carry):
        row_block = plan[slot, 0]
        col_block = plan[slot, 1]
        high = split[slot, 0]
        low = split[slot, 1]
        for source, target, dim, live in (
            (row_block, col_block, 0, None),
            (col_block, row_block, 1, row_block != col_block),
        ):
            dims = (((1,), (dim,)), ((), ()))
            both = err[source]
            lead = lax.dot_general(both, high, dims, preferred_element_type=jnp.float32)
            rest = lax.dot_general(both[:rows], low, dims, preferred_element_type=jnp.float32)
            term = lead[:rows] + (lead[rows:] + rest)
            if live is not None:
                term = jnp.where(live, term, 0.0)
            acc[target] += term
        return carry

    lax.fori_loop(0, split.shape[0], one_slot, 0, unroll=3)
    for p in range(count):
        for part, block, columns in places(me ^ p, order, width):
            outs[p][:, part] = acc[block, :, columns]


def product(plan, split, pieces):
    slots, _, order, _ = split.shape
    count = len(pieces)
    rows, width = pieces[0].shape
    blocks = count * width // order
    return pl.pallas_call(
        functools.partial(product_kernel, count),
        in_specs=[pl.BlockSpec(memory_space=pltpu.SMEM)] + [IN_VMEM] * (1 + count),
        out_specs=[IN_VMEM] * count,
        out_shape=[jax.ShapeDtypeStruct((rows, width), jnp.float32)] * count,
        scratch_shapes=[
            pltpu.VMEM((blocks, 2 * rows, order), jnp.bfloat16),
            pltpu.VMEM((blocks, rows, order), jnp.float32),
        ],
        compiler_params=pltpu.CompilerParams(vmem_limit_bytes=16 * MIB),
        cost_estimate=pl.CostEstimate(
            flops=slots * 12 * rows * order * order, bytes_accessed=8 * blocks * rows * order, transcendentals=0
        ),
        name="hessian_product",
    )(plan, pltpu.with_memory_space_constraint(split, pltpu.VMEM), *pieces)


def body(dense_weight, start_weight, keep_mask, tile_plan, hess_tiles):
    keep = keep_mask.astype(jnp.float32)
    weights = start_weight
    velocity = jnp.zeros(start_weight.shape, jnp.float32)
    split = split_tiles(hess_tiles)
    for step in range(ITERS):
        pieces = gather(weights - dense_weight)
        terms = scatter_sum(product(tile_plan, split, pieces))
        gradient = sum(terms[1:], terms[0])
        velocity = momentum * velocity + gradient
        weights = keep * (weights - step_size * velocity)
    return (weights, velocity)


def solution(mesh):
    placed = (
        P("layers", "col"),
        P("layers", "col"),
        P("layers", "col"),
        P(("layers", "col"), None),
        P(("layers", "col"), None, None),
    )
    return jax.shard_map(
        body,
        mesh=mesh,
        in_specs=placed,
        out_specs=(P("layers", "col"), P("layers", "col")),
        check_vma=False,
    )
```

```python
import functools

import jax
import jax.numpy as jnp
from jax import lax
from jax.experimental import pallas as pl
from jax.experimental.pallas import tpu as pltpu
from jax.sharding import PartitionSpec as P

ITERS = 2
MIB = 2**20
SCOPED = 24 * MIB
DEPTH = 3

step_size = 0.15
momentum = 0.6

IN_VMEM = pl.BlockSpec(memory_space=pltpu.VMEM)
IN_SMEM = pl.BlockSpec(memory_space=pltpu.SMEM)

CORE, HALF = 1, 2


def swap(x, mask):
    count = lax.axis_size("col")
    return lax.ppermute(x, "col", [(i, i ^ mask) for i in range(count)])


def far_bits(count):
    return [1 << i for i in range(2, count.bit_length() - 1)]


def far_pieces(count):
    return list(range(0, count, 4))


def gather(own):
    count = lax.axis_size("col")
    pieces = {0: own}
    for bit in reversed(far_bits(count)):
        for p in list(pieces):
            pieces[p | bit] = swap(pieces[p], bit)
    for p in sorted(pieces, key=lambda p: p.bit_count()):
        pieces[p | HALF] = swap(pieces[p], HALF)
    order = sorted(pieces, key=lambda p: p.bit_count())
    arrays = [([p], pieces[p][None]) for p in order]
    for start in range(0, len(order), 4):
        some = order[start : start + 4]
        arrays.append(([p | CORE for p in some], swap(jnp.stack([pieces[p] for p in some]), CORE)))
    return arrays


def scatter_sum(kept_half, sent_half, kept_own, sent_own):
    count = lax.axis_size("col")
    far = far_pieces(count)
    half = kept_half + swap(sent_half, CORE)
    crossed = {p: swap(half[j], HALF) for j, p in reversed(list(enumerate(far)))}
    own = kept_own + swap(sent_own, CORE)
    held = {p: own[j] + crossed[p] for j, p in enumerate(far)}
    for bit in far_bits(count):
        for p in sorted((p for p in held if p & bit), reverse=True):
            held[p ^ bit] += swap(held.pop(p), bit)
    return held[0]


def places(owner, order, width):
    if width >= order:
        each = width // order
        return [(slice(j * order, (j + 1) * order), owner * each + j, slice(None)) for j in range(each)]
    each = order // width
    start = pl.multiple_of(lax.rem(owner, each) * width, width)
    return [(slice(None), lax.div(owner, each), pl.ds(start, width))]


def take_pieces(held, pieces, err, order):
    me = lax.axis_index("col")
    _, rows, width = pieces[0].shape
    for places_held, ref in zip(held, pieces, strict=True):
        for i, p in enumerate(places_held):
            for part, block, columns in places(me ^ p, order, width):
                piece = ref[i, :, part]
                high = piece.astype(jnp.bfloat16)
                err[block, :rows, columns] = high
                err[block, rows:, columns] = (piece - high.astype(jnp.float32)).astype(jnp.bfloat16)


def give_sums(acc, outs, count, width, order):
    me = lax.axis_index("col")
    for out, offset in zip(outs, (HALF, HALF | CORE, 0, CORE), strict=True):
        for j, p in enumerate(far_pieces(count)):
            for part, block, columns in places(me ^ (p | offset), order, width):
                out[j, :, part] = acc[block, :, columns]


def add_products(row_block, col_block, high, low, err, acc):
    rows = acc.shape[1]
    for source, target, dim in ((row_block, col_block, 0), (col_block, row_block, 1)):
        dims = (((1,), (dim,)), ((), ()))
        both = err[source]
        lead = lax.dot_general(both, high, dims, preferred_element_type=jnp.float32)
        rest = lax.dot_general(both[:rows], low, dims, preferred_element_type=jnp.float32)
        term = lead[:rows] + (lead[rows:] + rest)
        if dim:
            term = jnp.where(row_block != col_block, term, 0.0)
        acc[target] += term


def product_kernel(held, width, together, plan, tiles, *refs):
    pieces = refs[: len(held)]
    *outs, err, acc, ring, arrived = refs[len(held) :]
    slots, order, _ = tiles.shape
    count = acc.shape[0] * order // width
    steps = slots // together
    depth = ring.shape[0]

    def fetch(step):
        at = lax.rem(step, depth)
        return pltpu.make_async_copy(tiles.at[pl.ds(step * together, together)], ring.at[at], arrived.at[at])

    for step in range(min(depth, steps)):
        fetch(step).start()
    take_pieces(held, pieces, err, order)
    acc[...] = jnp.zeros(acc.shape, jnp.float32)

    def one_step(step, carry):
        fetch(step).wait()
        for j in range(together):
            slot = step * together + j
            tile = ring[lax.rem(step, depth), j]
            high = tile.astype(jnp.bfloat16)
            low = (tile - high.astype(jnp.float32)).astype(jnp.bfloat16)
            add_products(plan[slot, 0], plan[slot, 1], high, low, err, acc)

        @pl.when(step + depth < steps)
        def _():
            fetch(step + depth).start()

        return carry

    lax.fori_loop(0, steps, one_step, 0)
    give_sums(acc, outs, count, width, order)


def product(plan, tiles, arrays):
    slots, order, _ = tiles.shape
    held = [p for p, _ in arrays]
    count = sum(len(p) for p in held)
    _, rows, width = arrays[0][1].shape
    blocks = count * width // order
    together = 3 if slots % 3 == 0 else 1
    some = jax.ShapeDtypeStruct((count // 4, rows, width), jnp.float32)
    return pl.pallas_call(
        functools.partial(product_kernel, held, width, together),
        in_specs=[IN_SMEM, pl.BlockSpec(memory_space=pl.ANY)] + [IN_VMEM] * len(held),
        out_specs=[IN_VMEM] * 4,
        out_shape=[some] * 4,
        scratch_shapes=[
            pltpu.VMEM((blocks, 2 * rows, order), jnp.bfloat16),
            pltpu.VMEM((blocks, rows, order), jnp.float32),
            pltpu.VMEM((DEPTH, together, order, order), jnp.float32),
            pltpu.SemaphoreType.DMA((DEPTH,)),
        ],
        compiler_params=pltpu.CompilerParams(vmem_limit_bytes=SCOPED),
        cost_estimate=pl.CostEstimate(
            flops=slots * 12 * rows * order * order, bytes_accessed=slots * order * order * 4, transcendentals=0
        ),
        name="product",
    )(plan, tiles, *[x for _, x in arrays])


def body(dense_weight, start_weight, keep_mask, tile_plan, hess_tiles):
    keep = keep_mask.astype(jnp.float32)
    weights = start_weight
    velocity = jnp.zeros(start_weight.shape, jnp.float32)
    for step in range(ITERS):
        terms = product(tile_plan, hess_tiles, gather(weights - dense_weight))
        gradient = scatter_sum(*terms)
        velocity = momentum * velocity + gradient
        weights = keep * (weights - step_size * velocity)
    return (weights, velocity)


def solution(mesh):
    placed = (
        P("layers", "col"),
        P("layers", "col"),
        P("layers", "col"),
        P(("layers", "col"), None),
        P(("layers", "col"), None, None),
    )
    return jax.shard_map(
        body,
        mesh=mesh,
        in_specs=placed,
        out_specs=(P("layers", "col"), P("layers", "col")),
        check_vma=False,
    )
```

```python
import functools

import jax
import jax.numpy as jnp
from jax import lax
from jax.experimental import pallas as pl
from jax.experimental.pallas import tpu as pltpu
from jax.sharding import PartitionSpec as P

ITERS = 2
MIB = 2**20
SCOPED = 24 * MIB
DEPTH = 3

step_size = 0.15
momentum = 0.6

IN_VMEM = pl.BlockSpec(memory_space=pltpu.VMEM)
IN_SMEM = pl.BlockSpec(memory_space=pltpu.SMEM)

CORE = 1
NEAR = (2, 4)


def near_masks(count):
    masks = [0]
    for bit in NEAR:
        masks += [m | bit for m in masks if bit < count]
    return masks[1:]


def far_bits(count):
    return [1 << i for i in range(1, count.bit_length() - 1) if 1 << i not in NEAR]


def sum_groups(count):
    return [list(range(count // 2, count, 2)), list(range(0, count // 2, 2))]


def swap(x, mask):
    count = lax.axis_size("col")
    return lax.ppermute(x, "col", [(i, i ^ mask) for i in range(count)])


def gather(own):
    count = lax.axis_size("col")
    pieces = {0: own}
    for bit in reversed(far_bits(count)):
        for p in list(pieces):
            pieces[p | bit] = swap(pieces[p], bit)
    for p in sorted(pieces):
        for mask in near_masks(count):
            pieces[p | mask] = swap(pieces[p], mask)
    order = sorted(pieces, key=lambda p: p.bit_count())
    arrays = [([p], pieces[p][None]) for p in order]
    for start in range(0, len(order), 4):
        some = order[start : start + 4]
        arrays.append(([p | CORE for p in some], swap(jnp.stack([pieces[p] for p in some]), CORE)))
    return arrays


def scatter_sum(sums):
    count = lax.axis_size("col")
    held = {}
    for group, kept, sent in zip(sum_groups(count), sums[::2], sums[1::2], strict=True):
        whole = kept + swap(sent, CORE)
        held |= {p: whole[j] for j, p in enumerate(group)}
    masks = near_masks(count)
    for p in sorted((p for p in held if not p & sum(NEAR)), reverse=True):
        for mask in reversed(masks):
            held[p] += swap(held.pop(p | mask), mask)
    for bit in far_bits(count):
        for p in sorted((p for p in held if p & bit), reverse=True):
            held[p ^ bit] += swap(held.pop(p), bit)
    return held[0]


def places(owner, order, width):
    if width >= order:
        each = width // order
        return [(slice(j * order, (j + 1) * order), owner * each + j, slice(None)) for j in range(each)]
    each = order // width
    start = pl.multiple_of(lax.rem(owner, each) * width, width)
    return [(slice(None), lax.div(owner, each), pl.ds(start, width))]


def take_pieces(held, pieces, err, order):
    me = lax.axis_index("col")
    _, rows, width = pieces[0].shape
    for places_held, ref in zip(held, pieces, strict=True):
        for i, p in enumerate(places_held):
            for part, block, columns in places(me ^ p, order, width):
                piece = ref[i, :, part]
                high = piece.astype(jnp.bfloat16)
                err[block, :rows, columns] = high
                err[block, rows:, columns] = (piece - high.astype(jnp.float32)).astype(jnp.bfloat16)


def give_sums(acc, outs, count, width, order):
    me = lax.axis_index("col")
    for g, group in enumerate(sum_groups(count)):
        for core in (0, CORE):
            for j, p in enumerate(group):
                for part, block, columns in places(me ^ (p | core), order, width):
                    outs[2 * g + core][j, :, part] = acc[block, :, columns]


def add_products(row_block, col_block, high, low, err, acc):
    rows = acc.shape[1]
    for source, target, dim in ((row_block, col_block, 0), (col_block, row_block, 1)):
        dims = (((1,), (dim,)), ((), ()))
        both = err[source]
        lead = lax.dot_general(both, high, dims, preferred_element_type=jnp.float32)
        rest = lax.dot_general(both[:rows], low, dims, preferred_element_type=jnp.float32)
        term = lead[:rows] + (lead[rows:] + rest)
        if dim:
            term = jnp.where(row_block != col_block, term, 0.0)
        acc[target] += term


def product_kernel(held, width, together, plan, tiles, *refs):
    pieces = refs[: len(held)]
    *outs, err, acc, ring, arrived = refs[len(held) :]
    slots, order, _ = tiles.shape
    count = acc.shape[0] * order // width
    steps = slots // together
    depth = ring.shape[0]

    def fetch(step):
        at = lax.rem(step, depth)
        return pltpu.make_async_copy(tiles.at[pl.ds(step * together, together)], ring.at[at], arrived.at[at])

    for step in range(min(depth, steps)):
        fetch(step).start()
    take_pieces(held, pieces, err, order)
    acc[...] = jnp.zeros(acc.shape, jnp.float32)

    def one_step(step, carry):
        fetch(step).wait()
        for j in range(together):
            slot = step * together + j
            tile = ring[lax.rem(step, depth), j]
            high = tile.astype(jnp.bfloat16)
            low = (tile - high.astype(jnp.float32)).astype(jnp.bfloat16)
            add_products(plan[slot, 0], plan[slot, 1], high, low, err, acc)

        @pl.when(step + depth < steps)
        def _():
            fetch(step + depth).start()

        return carry

    lax.fori_loop(0, steps, one_step, 0)
    give_sums(acc, outs, count, width, order)


def product(plan, tiles, arrays):
    slots, order, _ = tiles.shape
    held = [p for p, _ in arrays]
    count = sum(len(p) for p in held)
    _, rows, width = arrays[0][1].shape
    blocks = count * width // order
    together = 3 if slots % 3 == 0 else 1
    some = jax.ShapeDtypeStruct((count // 4, rows, width), jnp.float32)
    return pl.pallas_call(
        functools.partial(product_kernel, held, width, together),
        in_specs=[IN_SMEM, pl.BlockSpec(memory_space=pl.ANY)] + [IN_VMEM] * len(held),
        out_specs=[IN_VMEM] * 4,
        out_shape=[some] * 4,
        scratch_shapes=[
            pltpu.VMEM((blocks, 2 * rows, order), jnp.bfloat16),
            pltpu.VMEM((blocks, rows, order), jnp.float32),
            pltpu.VMEM((DEPTH, together, order, order), jnp.float32),
            pltpu.SemaphoreType.DMA((DEPTH,)),
        ],
        compiler_params=pltpu.CompilerParams(vmem_limit_bytes=SCOPED),
        cost_estimate=pl.CostEstimate(
            flops=slots * 12 * rows * order * order, bytes_accessed=slots * order * order * 4, transcendentals=0
        ),
        name="product",
    )(plan, tiles, *[x for _, x in arrays])


def body(dense_weight, start_weight, keep_mask, tile_plan, hess_tiles):
    keep = keep_mask.astype(jnp.float32)
    weights = start_weight
    velocity = jnp.zeros(start_weight.shape, jnp.float32)
    for step in range(ITERS):
        terms = product(tile_plan, hess_tiles, gather(weights - dense_weight))
        gradient = scatter_sum(terms)
        velocity = momentum * velocity + gradient
        weights = keep * (weights - step_size * velocity)
    return (weights, velocity)


def solution(mesh):
    placed = (
        P("layers", "col"),
        P("layers", "col"),
        P("layers", "col"),
        P(("layers", "col"), None),
        P(("layers", "col"), None, None),
    )
    return jax.shard_map(
        body,
        mesh=mesh,
        in_specs=placed,
        out_specs=(P("layers", "col"), P("layers", "col")),
        check_vma=False,
    )
```

```python
import functools

import jax
import jax.numpy as jnp
from jax import lax
from jax.experimental import pallas as pl
from jax.experimental.pallas import tpu as pltpu
from jax.sharding import PartitionSpec as P

ITERS = 2
MIB = 2**20
SCOPED = 24 * MIB
DEPTH = 6

step_size = 0.15
momentum = 0.6

IN_VMEM = pl.BlockSpec(memory_space=pltpu.VMEM)
IN_SMEM = pl.BlockSpec(memory_space=pltpu.SMEM)

CORE = 1
NEAR = (2, 4)


def near_masks(count):
    masks = [0]
    for bit in NEAR:
        masks += [m | bit for m in masks if bit < count]
    return masks[1:]


def far_bits(count):
    return [1 << i for i in range(1, count.bit_length() - 1) if 1 << i not in NEAR]


def sum_groups(count):
    return [list(range(count // 2, count, 2)), list(range(0, count // 2, 2))]


def swap(x, mask):
    count = lax.axis_size("col")
    return lax.ppermute(x, "col", [(i, i ^ mask) for i in range(count)])


def gather(own):
    count = lax.axis_size("col")
    pieces = {0: own}
    for bit in reversed(far_bits(count)):
        for p in list(pieces):
            pieces[p | bit] = swap(pieces[p], bit)
    for p in sorted(pieces):
        for mask in near_masks(count):
            pieces[p | mask] = swap(pieces[p], mask)
    order = sorted(pieces, key=lambda p: p.bit_count())
    arrays = [([p], pieces[p][None]) for p in order]
    for start in range(0, len(order), 4):
        some = order[start : start + 4]
        arrays.append(([p | CORE for p in some], swap(jnp.stack([pieces[p] for p in some]), CORE)))
    return arrays


def scatter_sum(sums):
    count = lax.axis_size("col")
    held = {}
    for group, kept, sent in zip(sum_groups(count), sums[::2], sums[1::2], strict=True):
        whole = kept + swap(sent, CORE)
        held |= {p: whole[j] for j, p in enumerate(group)}
    masks = near_masks(count)
    for p in sorted((p for p in held if not p & sum(NEAR)), reverse=True):
        for mask in reversed(masks):
            held[p] += swap(held.pop(p | mask), mask)
    for bit in far_bits(count):
        for p in sorted((p for p in held if p & bit), reverse=True):
            held[p ^ bit] += swap(held.pop(p), bit)
    return held[0]


def places(owner, order, width):
    if width >= order:
        each = width // order
        return [(slice(j * order, (j + 1) * order), owner * each + j, slice(None)) for j in range(each)]
    each = order // width
    start = pl.multiple_of(lax.rem(owner, each) * width, width)
    return [(slice(None), lax.div(owner, each), pl.ds(start, width))]


def take_pieces(held, pieces, err, order):
    me = lax.axis_index("col")
    _, rows, width = pieces[0].shape
    for places_held, ref in zip(held, pieces, strict=True):
        for i, p in enumerate(places_held):
            for part, block, columns in places(me ^ p, order, width):
                piece = ref[i, :, part]
                high = piece.astype(jnp.bfloat16)
                err[block, :rows, columns] = high
                err[block, rows:, columns] = (piece - high.astype(jnp.float32)).astype(jnp.bfloat16)


def give_sums(acc, outs, count, width, order):
    me = lax.axis_index("col")
    for g, group in enumerate(sum_groups(count)):
        for core in (0, CORE):
            for j, p in enumerate(group):
                for part, block, columns in places(me ^ (p | core), order, width):
                    outs[2 * g + core][j, :, part] = acc[block, :, columns]


def add_products(row_block, col_block, ready, err, acc):
    rows = acc.shape[1]

    def term(source, at):
        both = err[source]
        lead = jnp.dot(both, ready[at], preferred_element_type=jnp.float32)
        rest = jnp.dot(both[:rows], ready[at + 1], preferred_element_type=jnp.float32)
        return lead[:rows] + (lead[rows:] + rest)

    acc[col_block] += term(row_block, 0)
    acc[row_block] += jnp.where(row_block != col_block, term(col_block, 2), 0.0)


def split_tile(tile, ready):
    for at, x in ((0, tile), (2, tile.T)):
        high = x.astype(jnp.bfloat16)
        ready[at] = high
        ready[at + 1] = (x - high.astype(jnp.float32)).astype(jnp.bfloat16)


def product_kernel(held, width, plan, tiles, *refs):
    pieces = refs[: len(held)]
    *outs, err, acc, ring, arrived, even, odd = refs[len(held) :]
    slots, order, _ = tiles.shape
    count = acc.shape[0] * order // width
    depth = ring.shape[0]

    def fetch(slot):
        at = lax.rem(slot, depth)
        return pltpu.make_async_copy(tiles.at[slot], ring.at[at], arrived.at[at])

    def refill(slot):
        @pl.when(slot + depth < slots)
        def _():
            fetch(slot + depth).start()

    def prepare(slot, ready):
        split_tile(ring[lax.rem(slot, depth)], ready)

    def multiply(slot, ready):
        add_products(plan[slot, 0], plan[slot, 1], ready, err, acc)

    for slot in range(min(depth, slots)):
        fetch(slot).start()
    take_pieces(held, pieces, err, order)
    acc[...] = jnp.zeros(acc.shape, jnp.float32)
    fetch(0).wait()
    prepare(0, even)
    refill(0)

    def two_slots(step, carry):
        slot = 2 * step
        fetch(slot + 1).wait()
        fetch(slot + 2).wait()
        prepare(slot + 1, odd)
        multiply(slot, even)
        prepare(slot + 2, even)
        multiply(slot + 1, odd)
        refill(slot + 1)
        refill(slot + 2)
        return carry

    lax.fori_loop(0, (slots - 1) // 2, two_slots, 0)
    if slots % 2:
        multiply(slots - 1, even)
    else:
        fetch(slots - 1).wait()
        prepare(slots - 1, odd)
        multiply(slots - 2, even)
        multiply(slots - 1, odd)
    give_sums(acc, outs, count, width, order)


def product(plan, tiles, arrays):
    slots, order, _ = tiles.shape
    held = [p for p, _ in arrays]
    count = sum(len(p) for p in held)
    _, rows, width = arrays[0][1].shape
    blocks = count * width // order
    some = jax.ShapeDtypeStruct((count // 4, rows, width), jnp.float32)
    return pl.pallas_call(
        functools.partial(product_kernel, held, width),
        in_specs=[IN_SMEM, pl.BlockSpec(memory_space=pl.ANY)] + [IN_VMEM] * len(held),
        out_specs=[IN_VMEM] * 4,
        out_shape=[some] * 4,
        scratch_shapes=[
            pltpu.VMEM((blocks, 2 * rows, order), jnp.bfloat16),
            pltpu.VMEM((blocks, rows, order), jnp.float32),
            pltpu.VMEM((DEPTH, order, order), jnp.float32),
            pltpu.SemaphoreType.DMA((DEPTH,)),
            pltpu.VMEM((4, order, order), jnp.bfloat16),
            pltpu.VMEM((4, order, order), jnp.bfloat16),
        ],
        compiler_params=pltpu.CompilerParams(vmem_limit_bytes=SCOPED),
        cost_estimate=pl.CostEstimate(
            flops=slots * 12 * rows * order * order, bytes_accessed=slots * order * order * 4, transcendentals=0
        ),
        name="product",
    )(plan, tiles, *[x for _, x in arrays])


def body(dense_weight, start_weight, keep_mask, tile_plan, hess_tiles):
    keep = keep_mask.astype(jnp.float32)
    weights = start_weight
    velocity = jnp.zeros(start_weight.shape, jnp.float32)
    for step in range(ITERS):
        terms = product(tile_plan, hess_tiles, gather(weights - dense_weight))
        gradient = scatter_sum(terms)
        velocity = momentum * velocity + gradient
        weights = keep * (weights - step_size * velocity)
    return (weights, velocity)


def solution(mesh):
    placed = (
        P("layers", "col"),
        P("layers", "col"),
        P("layers", "col"),
        P(("layers", "col"), None),
        P(("layers", "col"), None, None),
    )
    return jax.shard_map(
        body,
        mesh=mesh,
        in_specs=placed,
        out_specs=(P("layers", "col"), P("layers", "col")),
        check_vma=False,
    )
```

```python
import functools

import jax
import jax.numpy as jnp
from jax import lax
from jax.experimental import pallas as pl
from jax.experimental.pallas import tpu as pltpu
from jax.sharding import PartitionSpec as P

ITERS = 2
MIB = 2**20
SCOPED = 24 * MIB
DEPTH = 6

step_size = 0.15
momentum = 0.6

IN_VMEM = pl.BlockSpec(memory_space=pltpu.VMEM)
IN_SMEM = pl.BlockSpec(memory_space=pltpu.SMEM)

CORE = 1
NEAR = (2, 4)


def far_bits(count):
    return [1 << i for i in range(1, count.bit_length() - 1) if 1 << i not in NEAR]


def sum_groups(count):
    return [list(range(count // 2, count, 2)), list(range(0, count // 2, 2))]


def swap(x, mask):
    count = lax.axis_size("col")
    return lax.ppermute(x, "col", [(i, i ^ mask) for i in range(count)])


def gather(own, corner_at_once):
    count = lax.axis_size("col")
    low, high = NEAR
    pieces = {0: own}
    far = [0]
    for bit in reversed(far_bits(count)):
        for p in list(far):
            pieces[p | bit] = swap(pieces[p], bit)
            far.append(p | bit)
    pieces[high] = swap(own, high)
    pieces[low] = swap(own, low)
    pieces[low | high] = swap(own, low | high) if corner_at_once else swap(pieces[high], low)
    for p in sorted(far[1:]):
        for mask in (high, low, low | high):
            pieces[p | mask] = swap(pieces[p], mask)
    order = sorted(pieces) if corner_at_once else sorted(pieces, key=lambda p: p.bit_count())
    arrays = [([p], pieces[p][None]) for p in order]
    for start in range(0, len(order), 4):
        some = order[start : start + 4]
        arrays.append(([p | CORE for p in some], swap(jnp.stack([pieces[p] for p in some]), CORE)))
    return arrays


def scatter_sum(sums):
    count = lax.axis_size("col")
    low, high = NEAR
    held = {}
    for group, kept, sent in zip(sum_groups(count), sums[::2], sums[1::2], strict=True):
        whole = kept + swap(sent, CORE)
        held |= {p: whole[j] for j, p in enumerate(group)}
    for p in sorted((p for p in held if not p & (low | high)), reverse=True):
        for mask in (low | high, high, low):
            held[p] += swap(held.pop(p | mask), mask)
    for bit in far_bits(count):
        for p in sorted((p for p in held if p & bit), reverse=True):
            held[p ^ bit] += swap(held.pop(p), bit)
    return held[0]


def places(owner, order, width):
    if width >= order:
        each = width // order
        return [(slice(j * order, (j + 1) * order), owner * each + j, slice(None)) for j in range(each)]
    each = order // width
    start = pl.multiple_of(lax.rem(owner, each) * width, width)
    return [(slice(None), lax.div(owner, each), pl.ds(start, width))]


def take_pieces(held, pieces, err, order):
    me = lax.axis_index("col")
    _, rows, width = pieces[0].shape
    for places_held, ref in zip(held, pieces, strict=True):
        for i, p in enumerate(places_held):
            for part, block, columns in places(me ^ p, order, width):
                piece = ref[i, :, part]
                high = piece.astype(jnp.bfloat16)
                err[block, :rows, columns] = high
                err[block, rows:, columns] = (piece - high.astype(jnp.float32)).astype(jnp.bfloat16)


def give_sums(acc, outs, count, width, order):
    me = lax.axis_index("col")
    for g, group in enumerate(sum_groups(count)):
        for core in (0, CORE):
            for j, p in enumerate(group):
                for part, block, columns in places(me ^ (p | core), order, width):
                    outs[2 * g + core][j, :, part] = acc[block, :, columns]


def add_products(row_block, col_block, ready, err, acc):
    rows = acc.shape[1]

    def term(source, at):
        both = err[source]
        lead = jnp.dot(both, ready[at], preferred_element_type=jnp.float32)
        rest = jnp.dot(both[:rows], ready[at + 1], preferred_element_type=jnp.float32)
        return lead[:rows] + (lead[rows:] + rest)

    acc[col_block] += term(row_block, 0)
    acc[row_block] += jnp.where(row_block != col_block, term(col_block, 2), 0.0)


def split_tile(tile, ready):
    for at, x in ((0, tile), (2, tile.T)):
        high = x.astype(jnp.bfloat16)
        ready[at] = high
        ready[at + 1] = (x - high.astype(jnp.float32)).astype(jnp.bfloat16)


def product_kernel(held, width, plan, tiles, *refs):
    pieces = refs[: len(held)]
    *outs, err, acc, ring, arrived, even, odd = refs[len(held) :]
    slots, order, _ = tiles.shape
    count = acc.shape[0] * order // width
    depth = ring.shape[0]

    def fetch(slot):
        at = lax.rem(slot, depth)
        return pltpu.make_async_copy(tiles.at[slot], ring.at[at], arrived.at[at])

    def refill(slot):
        @pl.when(slot + depth < slots)
        def _():
            fetch(slot + depth).start()

    def prepare(slot, ready):
        split_tile(ring[lax.rem(slot, depth)], ready)

    def multiply(slot, ready):
        add_products(plan[0, slot], plan[1, slot], ready, err, acc)

    for slot in range(min(depth, slots)):
        fetch(slot).start()
    take_pieces(held, pieces, err, order)
    acc[...] = jnp.zeros(acc.shape, jnp.float32)
    fetch(0).wait()
    prepare(0, even)
    refill(0)

    def two_slots(step, carry):
        slot = 2 * step
        fetch(slot + 1).wait()
        fetch(slot + 2).wait()
        prepare(slot + 1, odd)
        multiply(slot, even)
        prepare(slot + 2, even)
        multiply(slot + 1, odd)
        refill(slot + 1)
        refill(slot + 2)
        return carry

    lax.fori_loop(0, (slots - 1) // 2, two_slots, 0)
    if slots % 2:
        multiply(slots - 1, even)
    else:
        fetch(slots - 1).wait()
        prepare(slots - 1, odd)
        multiply(slots - 2, even)
        multiply(slots - 1, odd)
    give_sums(acc, outs, count, width, order)


def product(plan, tiles, arrays):
    slots, order, _ = tiles.shape
    held = [p for p, _ in arrays]
    count = sum(len(p) for p in held)
    _, rows, width = arrays[0][1].shape
    blocks = count * width // order
    some = jax.ShapeDtypeStruct((count // 4, rows, width), jnp.float32)
    return pl.pallas_call(
        functools.partial(product_kernel, held, width),
        in_specs=[IN_SMEM, pl.BlockSpec(memory_space=pl.ANY)] + [IN_VMEM] * len(held),
        out_specs=[IN_VMEM] * 4,
        out_shape=[some] * 4,
        scratch_shapes=[
            pltpu.VMEM((blocks, 2 * rows, order), jnp.bfloat16),
            pltpu.VMEM((blocks, rows, order), jnp.float32),
            pltpu.VMEM((DEPTH, order, order), jnp.float32),
            pltpu.SemaphoreType.DMA((DEPTH,)),
            pltpu.VMEM((4, order, order), jnp.bfloat16),
            pltpu.VMEM((4, order, order), jnp.bfloat16),
        ],
        compiler_params=pltpu.CompilerParams(vmem_limit_bytes=SCOPED),
        cost_estimate=pl.CostEstimate(
            flops=slots * 12 * rows * order * order, bytes_accessed=slots * order * order * 4, transcendentals=0
        ),
        name="product",
    )(plan, tiles, *[x for _, x in arrays])


def body(dense_weight, start_weight, keep_mask, tile_plan, hess_tiles):
    keep = keep_mask.astype(jnp.float32)
    weights = start_weight
    velocity = jnp.zeros(start_weight.shape, jnp.float32)
    for step in range(ITERS):
        terms = product(tile_plan.T, hess_tiles, gather(weights - dense_weight, step > 0))
        gradient = scatter_sum(terms)
        velocity = momentum * velocity + gradient
        weights = keep * (weights - step_size * velocity)
    return (weights, velocity)


def solution(mesh):
    placed = (
        P("layers", "col"),
        P("layers", "col"),
        P("layers", "col"),
        P(("layers", "col"), None),
        P(("layers", "col"), None, None),
    )
    return jax.shard_map(
        body,
        mesh=mesh,
        in_specs=placed,
        out_specs=(P("layers", "col"), P("layers", "col")),
        check_vma=False,
    )
```

```python
import functools

import jax
import jax.numpy as jnp
from jax import lax
from jax.experimental import pallas as pl
from jax.experimental.pallas import tpu as pltpu
from jax.sharding import PartitionSpec as P

ITERS = 2
MIB = 2**20
SCOPED = 24 * MIB
DEPTH = 6

step_size = 0.15
momentum = 0.6

IN_VMEM = pl.BlockSpec(memory_space=pltpu.VMEM)
IN_SMEM = pl.BlockSpec(memory_space=pltpu.SMEM)

CORE = 1
NEAR = (2, 4)


def far_bits(count):
    return [1 << i for i in range(1, count.bit_length() - 1) if 1 << i not in NEAR]


def sum_groups(count):
    return [list(range(count // 2, count, 2)), list(range(0, count // 2, 2))]


def swap(x, mask):
    count = lax.axis_size("col")
    return lax.ppermute(x, "col", [(i, i ^ mask) for i in range(count)])


def gather(own, corner_at_once):
    count = lax.axis_size("col")
    low, high = NEAR
    pieces = {0: own}
    far = [0]
    for bit in reversed(far_bits(count)):
        for p in list(far):
            pieces[p | bit] = swap(pieces[p], bit)
            far.append(p | bit)
    pieces[high] = swap(own, high)
    pieces[low] = swap(own, low)
    pieces[low | high] = swap(own, low | high) if corner_at_once else swap(pieces[high], low)
    for p in sorted(far[1:]):
        for mask in (low, high, low | high):
            pieces[p | mask] = swap(pieces[p], mask)
    order = sorted(pieces) if corner_at_once else sorted(pieces, key=lambda p: p.bit_count())
    arrays = [([p], pieces[p][None]) for p in order]
    for start in range(0, len(order), 4):
        some = order[start : start + 4]
        arrays.append(([p | CORE for p in some], swap(jnp.stack([pieces[p] for p in some]), CORE)))
    return arrays


def scatter_sum(sums):
    count = lax.axis_size("col")
    low, high = NEAR
    held = {}
    for group, kept, sent in zip(sum_groups(count), sums[::2], sums[1::2], strict=True):
        whole = kept + swap(sent, CORE)
        held |= {p: whole[j] for j, p in enumerate(group)}
    for p in sorted((p for p in held if not p & (low | high)), reverse=True):
        for mask in (low, low | high, high):
            held[p] += swap(held.pop(p | mask), mask)
    for bit in far_bits(count):
        for p in sorted((p for p in held if p & bit), reverse=True):
            held[p ^ bit] += swap(held.pop(p), bit)
    return held[0]


def places(owner, order, width):
    if width >= order:
        each = width // order
        return [(slice(j * order, (j + 1) * order), owner * each + j, slice(None)) for j in range(each)]
    each = order // width
    start = pl.multiple_of(lax.rem(owner, each) * width, width)
    return [(slice(None), lax.div(owner, each), pl.ds(start, width))]


def take_pieces(held, pieces, err, order):
    me = lax.axis_index("col")
    _, rows, width = pieces[0].shape
    for places_held, ref in zip(held, pieces, strict=True):
        for i, p in enumerate(places_held):
            for part, block, columns in places(me ^ p, order, width):
                piece = ref[i, :, part]
                high = piece.astype(jnp.bfloat16)
                err[block, :rows, columns] = high
                err[block, rows:, columns] = (piece - high.astype(jnp.float32)).astype(jnp.bfloat16)


def give_sums(acc, outs, count, width, order):
    me = lax.axis_index("col")
    for g, group in enumerate(sum_groups(count)):
        for core in (0, CORE):
            for j, p in enumerate(group):
                for part, block, columns in places(me ^ (p | core), order, width):
                    outs[2 * g + core][j, :, part] = acc[block, :, columns]


def add_products(row_block, col_block, ready, err, acc):
    rows = acc.shape[1]

    def term(source, at):
        both = err[source]
        lead = jnp.dot(both, ready[at], preferred_element_type=jnp.float32)
        rest = jnp.dot(both[:rows], ready[at + 1], preferred_element_type=jnp.float32)
        return lead[:rows] + (lead[rows:] + rest)

    acc[col_block] += term(row_block, 0)
    acc[row_block] += jnp.where(row_block != col_block, term(col_block, 2), 0.0)


def split_tile(tile, ready):
    for at, x in ((0, tile), (2, tile.T)):
        high = x.astype(jnp.bfloat16)
        ready[at] = high
        ready[at + 1] = (x - high.astype(jnp.float32)).astype(jnp.bfloat16)


def product_kernel(held, width, plan, tiles, *refs):
    pieces = refs[: len(held)]
    *outs, err, acc, ring, arrived, even, odd = refs[len(held) :]
    slots, order, _ = tiles.shape
    count = acc.shape[0] * order // width
    depth = ring.shape[0]

    def fetch(slot):
        at = lax.rem(slot, depth)
        return pltpu.make_async_copy(tiles.at[slot], ring.at[at], arrived.at[at])

    def refill(slot):
        @pl.when(slot + depth < slots)
        def _():
            fetch(slot + depth).start()

    def prepare(slot, ready):
        split_tile(ring[lax.rem(slot, depth)], ready)

    def multiply(slot, ready):
        add_products(plan[0, slot], plan[1, slot], ready, err, acc)

    for slot in range(min(depth, slots)):
        fetch(slot).start()
    take_pieces(held, pieces, err, order)
    acc[...] = jnp.zeros(acc.shape, jnp.float32)
    fetch(0).wait()
    prepare(0, even)
    refill(0)

    def two_slots(step, carry):
        slot = 2 * step
        fetch(slot + 1).wait()
        fetch(slot + 2).wait()
        prepare(slot + 1, odd)
        multiply(slot, even)
        prepare(slot + 2, even)
        multiply(slot + 1, odd)
        refill(slot + 1)
        refill(slot + 2)
        return carry

    lax.fori_loop(0, (slots - 1) // 2, two_slots, 0)
    if slots % 2:
        multiply(slots - 1, even)
    else:
        fetch(slots - 1).wait()
        prepare(slots - 1, odd)
        multiply(slots - 2, even)
        multiply(slots - 1, odd)
    give_sums(acc, outs, count, width, order)


def product(plan, tiles, arrays):
    slots, order, _ = tiles.shape
    held = [p for p, _ in arrays]
    count = sum(len(p) for p in held)
    _, rows, width = arrays[0][1].shape
    blocks = count * width // order
    some = jax.ShapeDtypeStruct((count // 4, rows, width), jnp.float32)
    return pl.pallas_call(
        functools.partial(product_kernel, held, width),
        in_specs=[IN_SMEM, pl.BlockSpec(memory_space=pl.ANY)] + [IN_VMEM] * len(held),
        out_specs=[IN_VMEM] * 4,
        out_shape=[some] * 4,
        scratch_shapes=[
            pltpu.VMEM((blocks, 2 * rows, order), jnp.bfloat16),
            pltpu.VMEM((blocks, rows, order), jnp.float32),
            pltpu.VMEM((DEPTH, order, order), jnp.float32),
            pltpu.SemaphoreType.DMA((DEPTH,)),
            pltpu.VMEM((4, order, order), jnp.bfloat16),
            pltpu.VMEM((4, order, order), jnp.bfloat16),
        ],
        compiler_params=pltpu.CompilerParams(vmem_limit_bytes=SCOPED),
        cost_estimate=pl.CostEstimate(
            flops=slots * 12 * rows * order * order, bytes_accessed=slots * order * order * 4, transcendentals=0
        ),
        name="product",
    )(plan, tiles, *[x for _, x in arrays])


def body(dense_weight, start_weight, keep_mask, tile_plan, hess_tiles):
    keep = keep_mask.astype(jnp.float32)
    weights = start_weight
    velocity = jnp.zeros(start_weight.shape, jnp.float32)
    for step in range(ITERS):
        terms = product(tile_plan.T, hess_tiles, gather(weights - dense_weight, step > 0))
        gradient = scatter_sum(terms)
        velocity = momentum * velocity + gradient
        weights = keep * (weights - step_size * velocity)
    return (weights, velocity)


def solution(mesh):
    placed = (
        P("layers", "col"),
        P("layers", "col"),
        P("layers", "col"),
        P(("layers", "col"), None),
        P(("layers", "col"), None, None),
    )
    return jax.shard_map(
        body,
        mesh=mesh,
        in_specs=placed,
        out_specs=(P("layers", "col"), P("layers", "col")),
        check_vma=False,
    )
```

```python
import functools

import jax
import jax.numpy as jnp
from jax import lax
from jax.experimental import pallas as pl
from jax.experimental.pallas import tpu as pltpu
from jax.sharding import PartitionSpec as P

ITERS = 2
MIB = 2**20
SCOPED = 24 * MIB
DEPTH = 6

step_size = 0.15
momentum = 0.6

IN_VMEM = pl.BlockSpec(memory_space=pltpu.VMEM)
IN_SMEM = pl.BlockSpec(memory_space=pltpu.SMEM)

CORE = 1
NEAR = (2, 4)


def far_bits(count):
    return [1 << i for i in range(1, count.bit_length() - 1) if 1 << i not in NEAR]


def sum_groups(count):
    return [list(range(count // 2, count, 2)), list(range(0, count // 2, 2))]


def swap(x, mask):
    count = lax.axis_size("col")
    return lax.ppermute(x, "col", [(i, i ^ mask) for i in range(count)])


def gather(own, corner_at_once):
    count = lax.axis_size("col")
    low, high = NEAR
    pieces = {0: own}
    far = [0]
    for bit in reversed(far_bits(count)):
        for p in list(far):
            pieces[p | bit] = swap(pieces[p], bit)
            far.append(p | bit)
    pieces[low] = swap(own, low)
    pieces[high] = swap(own, high)
    pieces[low | high] = swap(own, low | high) if corner_at_once else swap(pieces[high], low)
    for p in sorted(far[1:]):
        for mask in (low, high, low | high):
            pieces[p | mask] = swap(pieces[p], mask)
    order = sorted(pieces) if corner_at_once else sorted(pieces, key=lambda p: p.bit_count())
    arrays = [([p], pieces[p][None]) for p in order]
    for start in range(0, len(order), 4):
        some = order[start : start + 4]
        arrays.append(([p | CORE for p in some], swap(jnp.stack([pieces[p] for p in some]), CORE)))
    return arrays


def scatter_sum(sums):
    count = lax.axis_size("col")
    low, high = NEAR
    held = {}
    for group, kept, sent in zip(sum_groups(count), sums[::2], sums[1::2], strict=True):
        whole = kept + swap(sent, CORE)
        held |= {p: whole[j] for j, p in enumerate(group)}
    for p in sorted((p for p in held if not p & (low | high)), reverse=True):
        for mask in (low, low | high, high):
            held[p] += swap(held.pop(p | mask), mask)
    for bit in far_bits(count):
        for p in sorted((p for p in held if p & bit), reverse=True):
            held[p ^ bit] += swap(held.pop(p), bit)
    return held[0]


def places(owner, order, width):
    if width >= order:
        each = width // order
        return [(slice(j * order, (j + 1) * order), owner * each + j, slice(None)) for j in range(each)]
    each = order // width
    start = pl.multiple_of(lax.rem(owner, each) * width, width)
    return [(slice(None), lax.div(owner, each), pl.ds(start, width))]


def take_pieces(held, pieces, err, order):
    me = lax.axis_index("col")
    _, rows, width = pieces[0].shape
    for places_held, ref in zip(held, pieces, strict=True):
        for i, p in enumerate(places_held):
            for part, block, columns in places(me ^ p, order, width):
                piece = ref[i, :, part]
                high = piece.astype(jnp.bfloat16)
                err[block, :rows, columns] = high
                err[block, rows:, columns] = (piece - high.astype(jnp.float32)).astype(jnp.bfloat16)


def give_sums(acc, outs, count, width, order):
    me = lax.axis_index("col")
    for g, group in enumerate(sum_groups(count)):
        for core in (0, CORE):
            for j, p in enumerate(group):
                for part, block, columns in places(me ^ (p | core), order, width):
                    outs[2 * g + core][j, :, part] = acc[block, :, columns]


def add_products(row_block, col_block, ready, err, acc):
    rows = acc.shape[1]

    def term(source, at):
        both = err[source]
        lead = jnp.dot(both, ready[at], preferred_element_type=jnp.float32)
        rest = jnp.dot(both[:rows], ready[at + 1], preferred_element_type=jnp.float32)
        return lead[:rows] + (lead[rows:] + rest)

    acc[col_block] += term(row_block, 0)
    acc[row_block] += jnp.where(row_block != col_block, term(col_block, 2), 0.0)


def split_tile(tile, ready):
    for at, x in ((0, tile), (2, tile.T)):
        high = x.astype(jnp.bfloat16)
        ready[at] = high
        ready[at + 1] = (x - high.astype(jnp.float32)).astype(jnp.bfloat16)


def product_kernel(held, width, plan, tiles, *refs):
    pieces = refs[: len(held)]
    *outs, err, acc, ring, arrived, even, odd = refs[len(held) :]
    slots, order, _ = tiles.shape
    count = acc.shape[0] * order // width
    depth = ring.shape[0]

    def fetch(slot):
        at = lax.rem(slot, depth)
        return pltpu.make_async_copy(tiles.at[slot], ring.at[at], arrived.at[at])

    def refill(slot):
        @pl.when(slot + depth < slots)
        def _():
            fetch(slot + depth).start()

    def prepare(slot, ready):
        split_tile(ring[lax.rem(slot, depth)], ready)

    def multiply(slot, ready):
        add_products(plan[0, slot], plan[1, slot], ready, err, acc)

    for slot in range(min(depth, slots)):
        fetch(slot).start()
    take_pieces(held, pieces, err, order)
    acc[...] = jnp.zeros(acc.shape, jnp.float32)
    fetch(0).wait()
    prepare(0, even)
    refill(0)

    def two_slots(step, carry):
        slot = 2 * step
        fetch(slot + 1).wait()
        fetch(slot + 2).wait()
        prepare(slot + 1, odd)
        multiply(slot, even)
        prepare(slot + 2, even)
        multiply(slot + 1, odd)
        refill(slot + 1)
        refill(slot + 2)
        return carry

    lax.fori_loop(0, (slots - 1) // 2, two_slots, 0)
    if slots % 2:
        multiply(slots - 1, even)
    else:
        fetch(slots - 1).wait()
        prepare(slots - 1, odd)
        multiply(slots - 2, even)
        multiply(slots - 1, odd)
    give_sums(acc, outs, count, width, order)


def product(plan, tiles, arrays):
    slots, order, _ = tiles.shape
    held = [p for p, _ in arrays]
    count = sum(len(p) for p in held)
    _, rows, width = arrays[0][1].shape
    blocks = count * width // order
    some = jax.ShapeDtypeStruct((count // 4, rows, width), jnp.float32)
    return pl.pallas_call(
        functools.partial(product_kernel, held, width),
        in_specs=[IN_SMEM, pl.BlockSpec(memory_space=pl.ANY)] + [IN_VMEM] * len(held),
        out_specs=[IN_VMEM] * 4,
        out_shape=[some] * 4,
        scratch_shapes=[
            pltpu.VMEM((blocks, 2 * rows, order), jnp.bfloat16),
            pltpu.VMEM((blocks, rows, order), jnp.float32),
            pltpu.VMEM((DEPTH, order, order), jnp.float32),
            pltpu.SemaphoreType.DMA((DEPTH,)),
            pltpu.VMEM((4, order, order), jnp.bfloat16),
            pltpu.VMEM((4, order, order), jnp.bfloat16),
        ],
        compiler_params=pltpu.CompilerParams(vmem_limit_bytes=SCOPED),
        cost_estimate=pl.CostEstimate(
            flops=slots * 12 * rows * order * order, bytes_accessed=slots * order * order * 4, transcendentals=0
        ),
        name="product",
    )(plan, tiles, *[x for _, x in arrays])


def body(dense_weight, start_weight, keep_mask, tile_plan, hess_tiles):
    keep = keep_mask.astype(jnp.float32)
    weights = start_weight
    velocity = jnp.zeros(start_weight.shape, jnp.float32)
    for step in range(ITERS):
        terms = product(tile_plan.T, hess_tiles, gather(weights - dense_weight, step > 0))
        gradient = scatter_sum(terms)
        velocity = momentum * velocity + gradient
        weights = keep * (weights - step_size * velocity)
    return (weights, velocity)


def solution(mesh):
    placed = (
        P("layers", "col"),
        P("layers", "col"),
        P("layers", "col"),
        P(("layers", "col"), None),
        P(("layers", "col"), None, None),
    )
    return jax.shard_map(
        body,
        mesh=mesh,
        in_specs=placed,
        out_specs=(P("layers", "col"), P("layers", "col")),
        check_vma=False,
    )
```
